256 devices in a mesh: dp: 16 (over z_hi, x), seq: 16 (over y, z_lo, core).
Axes of the slice: x: 4, y: 4, z: 8 (z_hi: 4, z_lo: 2; z = z_hi * 2 + z_lo), core: 2. Of those that a mesh axis runs over, the one named last changes fastest.
Arguments:
- activations: bfloat16 [32768, 4096], P(('dp', 'seq')), may hold values from -24 to 24
- queries: bfloat16 [32768, 4096], P(('dp', 'seq')), may hold values from -130 to 130
- saved_keys: bfloat16 [32768, 256], P(('dp', 'seq')), may hold values from -6 to 6
- saved_values: bfloat16 [32768, 256], P(('dp', 'seq')), may hold values from -6 to 6
- output_gradient: bfloat16 [32768, 4096], P(('dp', 'seq')), may hold values from -6 to 6
- segments: int32 [16, 2048], P('dp'), may hold values from 0 to 5, never falling along the last dimension, each value on 1 to 1024 neighbouring positions
- weight_codes: int32 [4096, 512], P(('dp', 'seq')), may hold values from 32 to 215, as said below
- exponents: int32 [32, 4], replicated, may hold values from -8 to -6
Outputs:
- grad_q: bfloat16 [32768, 4096], P(('dp', 'seq'))
- grad_x: bfloat16 [32768, 4096], P(('dp', 'seq'))
- grad_weights: float32 [4096, 512], P(('dp', 'seq'))
The draws below stay inside these ranges and needn't reach their ends.
Inputs may be any that keep to these rules, and one draw needn't show every extreme that they name: `segments`: document ids never fall along a sequence; a document holds at most 1024 positions. `weight_codes`: each code c holds an FP8 E4M3 number with sign s = c // 128, exponent field e = (c // 8) % 16 from 4 to 10 and mantissa m = c % 8.
All inputs are finite; a program needn't handle non-finite values.
Results may differ from the reference program's by a relative error of at most 0.013.
Values may be sent and summed in bfloat16 or wider, within the bound.
No kernel may reach another device: no remote copies, remote signals or barrier semaphores. Data moves between devices by JAX's collectives and lax.ppermute only.
A program may use at most 128 MiB of HBM per device.

```python
import math
import jax
import jax.numpy as jnp
import numpy as np
from jax import lax

MODEL_WIDTH = 4096
QUERY_HEADS = 32
KEY_VALUE_HEADS = 2
HEAD_WIDTH = 128
SCALE_BLOCK_SIDE = 128
SEQUENCE_LENGTH = 2048
TOTAL_TOKENS = 32768
N_DP = 16


def base_keys(key):
    return jnp.clip(jax.random.normal(key, (TOTAL_TOKENS, KEY_VALUE_HEADS * HEAD_WIDTH), jnp.float32), -6.0, 6.0)


def draw_saved_keys(key, part):
    shared_heads = base_keys(key)
    return shared_heads.astype(jnp.bfloat16)


def draw_queries(key, part):
    key = jax.random.fold_in(key, 7)
    result = jnp.clip(jax.random.normal(key, (TOTAL_TOKENS, QUERY_HEADS * HEAD_WIDTH), jnp.float32), -6.0, 6.0)
    return result.astype(jnp.bfloat16)


def draw_weight_codes(key, part):
    key = jax.random.fold_in(key, 3)
    key_sign, key_expo, key_mant = jax.random.split(key, 3)
    array_shape = (MODEL_WIDTH, 2 * KEY_VALUE_HEADS * HEAD_WIDTH)
    sign_bit = jax.random.randint(key_sign, array_shape, 0, 2, dtype=jnp.int32)
    exponent_field = jax.random.randint(key_expo, array_shape, 4, 11, dtype=jnp.int32)
    mantissa = jax.random.randint(key_mant, array_shape, 0, 8, dtype=jnp.int32)
    return sign_bit * 128 + exponent_field * 8 + mantissa


def place_ends(values, stream_key, least, high):
    spot = [jax.random.randint(jax.random.fold_in(stream_key, axis), (), 0, length) for axis, length in enumerate(values.shape)]
    longest = values.shape.index(max(values.shape))
    next_to = spot[:longest] + [(spot[longest] + 1) % values.shape[longest]] + spot[longest + 1:]
    return values.at[tuple(spot)].set(least).at[tuple(next_to)].set(high)


def with_spikes(entries, key, source, target, shards_of, factor):
    owner, partner = [(jnp.arange(entries.shape[dim]) // (entries.shape[dim] // shards_of)).reshape([-1 if axis == dim else 1 for axis in range(entries.ndim)]) for dim in (source, target)]
    chosen = jax.random.permutation(key, shards_of)[partner]
    strong = (owner == chosen) | (owner == (partner + shards_of // 2) % shards_of)
    return jnp.where(strong, factor * entries, entries)


def levels(rng, extent, cuts, low, high):
    level = 1.0
    for axis_at, blocks in cuts:
        draws = jax.random.uniform(jax.random.fold_in(jax.random.fold_in(rng, 6), axis_at), (blocks,), jnp.float32, low / len(cuts), high / len(cuts))
        level = level * jnp.repeat(jnp.exp(draws), extent[axis_at] // blocks).reshape((-1,) + (1,) * (len(extent) - 1 - axis_at))
    return level


def length_profile(amount, total, bound, lean):
    portions = [(1 << 20) // math.isqrt(standing ** lean) + 1 for standing in range(2, amount + 1)]
    surplus, given = total - bound - (amount - 1), [1] * (amount - 1)
    while surplus > 0:
        movable = [i for i in range(amount - 1) if given[i] < bound]
        pool, left = sum([portions[i] for i in movable]), surplus
        for i in movable:
            addition = min(bound - given[i], max(1, left * portions[i] // pool), surplus)
            given[i] = given[i] + addition
            surplus = surplus - addition
    return np.array([bound] + given)


def ragged(key, number_of, total, limit, slope):
    if number_of == 2:
        one = jax.random.randint(key, (), max(1, total - limit), min(limit, total - 1) + 1)
        return jnp.stack([one, total - one])
    sizes = jnp.asarray(length_profile(number_of, total, limit, slope), jnp.int32)
    pairs = (number_of - 1) // 2
    giver, sink = sizes[1:1 + 2 * pairs:2], sizes[2:2 + 2 * pairs:2]
    room = jnp.minimum(giver - 1, limit - sink)
    passed = jax.random.randint(jax.random.fold_in(key, 1), (pairs,), 0, 1 << 20) % (room + 1)
    sizes = sizes.at[1:1 + 2 * pairs:2].set(giver - passed).at[2:2 + 2 * pairs:2].set(sink + passed)
    return sizes[jax.random.permutation(jax.random.fold_in(key, 2), number_of)]


def normal_values(rng, extent, width, reach, cuts=(), kind=jnp.bfloat16):
    entries = jax.random.normal(rng, extent, jnp.float32) * width
    if len(cuts) > 0:
        entries = levels(rng, extent, cuts, -0.22, 0.18) * entries
    return jnp.clip(entries, min=-reach, max=reach).astype(kind)


def noise_with(own_key, dims, spread, most, pieces, heavy, held_as=jnp.bfloat16):
    drawn = spread * jax.random.normal(own_key, dims, jnp.float32)
    if pieces:
        drawn = drawn * levels(own_key, dims, pieces, -0.22, 0.18)
    return jnp.clip(with_spikes(drawn, jax.random.fold_in(own_key, 3), *heavy), -most, most).astype(held_as)


def setup_inputs(seed: int = 0) -> dict:
    keys = jax.random.split(jax.random.key(seed), 9)
    activations = noise_with(keys[0], (TOTAL_TOKENS, MODEL_WIDTH), 1.0, 24.0, ((0, 256),), (0, 1, 256, 6.0))
    queries = draw_queries(jax.random.fold_in(keys[8], 71), 0)
    saved_keys = draw_saved_keys(jax.random.fold_in(keys[8], 71), 0)
    saved_values = normal_values(keys[3], (TOTAL_TOKENS, KEY_VALUE_HEADS * HEAD_WIDTH), 1.0, 6.0, ((0, 256),))
    output_gradient = normal_values(keys[4], (TOTAL_TOKENS, QUERY_HEADS * HEAD_WIDTH), 1.0, 6.0, ((0, 256),))
    segments = jax.vmap(lambda own: jnp.searchsorted(jnp.cumsum(ragged(own, 6, SEQUENCE_LENGTH, SEQUENCE_LENGTH // 2, 0)), jnp.arange(SEQUENCE_LENGTH), side="right"))(jax.random.split(keys[5], N_DP)).reshape((N_DP, SEQUENCE_LENGTH)).astype(jnp.int32)
    weight_codes = draw_weight_codes(jax.random.fold_in(keys[8], 71), 0)
    exponents = place_ends(jax.random.randint(keys[7], (MODEL_WIDTH // SCALE_BLOCK_SIDE, 2 * KEY_VALUE_HEADS * HEAD_WIDTH // SCALE_BLOCK_SIDE), -8, -5), jax.random.fold_in(keys[7], 1), -8, (-5) - 1).astype(jnp.int32)
    return dict(activations=activations, queries=queries, saved_keys=saved_keys, saved_values=saved_values, output_gradient=output_gradient, segments=segments, weight_codes=weight_codes, exponents=exponents)


masked_score = -1e+30

def decode_weights(weight_codes, exponents):
    sign_bit = (weight_codes // 128).astype(jnp.float32)
    exponent_field = (weight_codes // 8 % 16).astype(jnp.float32)
    mantissa = (weight_codes % 8).astype(jnp.float32)
    magnitude = jnp.exp2(exponent_field - 7.0) * (1.0 + mantissa / 8.0)
    block_scale = jnp.exp2(exponents.astype(jnp.float32))
    block_scale = jnp.repeat(jnp.repeat(block_scale, SCALE_BLOCK_SIDE, axis=0), SCALE_BLOCK_SIDE, axis=1)
    return ((1.0 - 2.0 * sign_bit) * magnitude * block_scale).astype(jnp.bfloat16)

def head_grads(query_head, key_head, value_head, grad_head, allowed):
    score_scale = 1.0 / math.sqrt(HEAD_WIDTH)
    scores = jnp.dot(query_head, key_head.T, preferred_element_type=jnp.float32) * score_scale
    scores = jnp.where(allowed, scores, masked_score)
    row_max = lax.optimization_barrier(jnp.max(scores, axis=-1, keepdims=True))
    exp_scores = jnp.exp(scores - row_max)
    soft_probs = exp_scores / lax.optimization_barrier(jnp.sum(exp_scores, axis=-1, keepdims=True))
    probs_bf = soft_probs.astype(jnp.bfloat16)
    attended = jnp.dot(probs_bf, value_head, preferred_element_type=jnp.float32)
    row_delta = lax.optimization_barrier(jnp.sum(grad_head.astype(jnp.float32) * attended, axis=-1, keepdims=True))
    dprobs = jnp.dot(grad_head, value_head.T, preferred_element_type=jnp.float32)
    dscores = (soft_probs * (dprobs - row_delta)).astype(jnp.bfloat16)
    grad_query = (score_scale * jnp.dot(dscores, key_head, preferred_element_type=jnp.float32)).astype(jnp.bfloat16)
    key_gradient = score_scale * jnp.dot(dscores.T, query_head, preferred_element_type=jnp.float32)
    value_gradient = jnp.dot(probs_bf.T, grad_head, preferred_element_type=jnp.float32)
    return (grad_query, key_gradient, value_gradient)

def sequence_grads(queries_seq, sequence_keys, sequence_values, grad_seq, doc_ids):
    positions = jnp.arange(SEQUENCE_LENGTH, dtype=jnp.int32)
    allowed = (positions[:, None] >= positions[None, :]) & (doc_ids[:, None] == doc_ids[None, :])
    head_group = QUERY_HEADS // KEY_VALUE_HEADS
    query_heads = queries_seq.reshape(SEQUENCE_LENGTH, QUERY_HEADS, HEAD_WIDTH).transpose(1, 0, 2)
    grad_heads = grad_seq.reshape(SEQUENCE_LENGTH, QUERY_HEADS, HEAD_WIDTH).transpose(1, 0, 2)
    heads_of_key = sequence_keys.reshape(SEQUENCE_LENGTH, KEY_VALUE_HEADS, HEAD_WIDTH).transpose(1, 0, 2)
    heads_of_value = sequence_values.reshape(SEQUENCE_LENGTH, KEY_VALUE_HEADS, HEAD_WIDTH).transpose(1, 0, 2)

    def one_head(head_idx):
        kv_idx = head_idx // head_group
        return head_grads(query_heads[head_idx], heads_of_key[kv_idx], heads_of_value[kv_idx], grad_heads[head_idx], allowed)
    grad_query, key_gradient, value_gradient = lax.map(one_head, jnp.arange(QUERY_HEADS, dtype=jnp.int32))
    grad_query = grad_query.transpose(1, 0, 2).reshape(SEQUENCE_LENGTH, QUERY_HEADS * HEAD_WIDTH)
    key_total = key_gradient.reshape(KEY_VALUE_HEADS, head_group, SEQUENCE_LENGTH, HEAD_WIDTH).sum(axis=1).transpose(1, 0, 2).reshape(SEQUENCE_LENGTH, KEY_VALUE_HEADS * HEAD_WIDTH)
    value_total = value_gradient.reshape(KEY_VALUE_HEADS, head_group, SEQUENCE_LENGTH, HEAD_WIDTH).sum(axis=1).transpose(1, 0, 2).reshape(SEQUENCE_LENGTH, KEY_VALUE_HEADS * HEAD_WIDTH)
    kv_grad = jnp.concatenate([key_total, value_total], axis=1).astype(jnp.bfloat16)
    return (grad_query, kv_grad)

def reference(activations, queries, saved_keys, saved_values, output_gradient, segments, weight_codes, exponents):
    weights = decode_weights(weight_codes, exponents)
    stacked_heads = (activations.reshape(N_DP, SEQUENCE_LENGTH, MODEL_WIDTH), queries.reshape(N_DP, SEQUENCE_LENGTH, QUERY_HEADS * HEAD_WIDTH), saved_keys.reshape(N_DP, SEQUENCE_LENGTH, KEY_VALUE_HEADS * HEAD_WIDTH), saved_values.reshape(N_DP, SEQUENCE_LENGTH, KEY_VALUE_HEADS * HEAD_WIDTH), output_gradient.reshape(N_DP, SEQUENCE_LENGTH, QUERY_HEADS * HEAD_WIDTH), segments)

    def one_seq(carry, items):
        act_seq, query_seq, key_seq, value_seq, grad_seq, doc_ids = items
        grad_query, kv_grad = sequence_grads(query_seq, key_seq, value_seq, grad_seq, doc_ids)
        grad_act = jnp.dot(kv_grad, weights.T, preferred_element_type=jnp.float32).astype(jnp.bfloat16)
        carry = carry + jnp.dot(act_seq.T, kv_grad, preferred_element_type=jnp.float32)
        return (carry, (grad_query, grad_act))
    initial_carry = jnp.zeros((MODEL_WIDTH, 2 * KEY_VALUE_HEADS * HEAD_WIDTH), jnp.float32)
    grad_weights, outs = lax.scan(one_seq, initial_carry, stacked_heads)
    grad_q = outs[0].reshape(TOTAL_TOKENS, QUERY_HEADS * HEAD_WIDTH)
    grad_x = outs[1].reshape(TOTAL_TOKENS, MODEL_WIDTH)
    return (grad_q, grad_x, grad_weights)
```

```python
import math

import jax
import jax.numpy as jnp
from jax import lax
from jax.experimental import pallas as pl
from jax.experimental.pallas import tpu as pltpu
from jax.sharding import PartitionSpec as P

QUERY_HEADS = 32
KEY_VALUE_HEADS = 2
HEAD_WIDTH = 128
SCALE_BLOCK_SIDE = 128
GROUP_HEADS = QUERY_HEADS // KEY_VALUE_HEADS
GROUP_COLS = GROUP_HEADS * HEAD_WIDTH
DOC_LIMIT = 1024
HEADS_STEP = 4

masked_bias = -1e30
score_scale = 1.0 / math.sqrt(HEAD_WIDTH)
exp2_scale = score_scale * math.log2(math.e)

NT = (((1,), (1,)), ((), ()))
NN = (((1,), (0,)), ((), ()))


def dot(a, b, dims):
    return lax.dot_general(a, b, dims, preferred_element_type=jnp.float32)


def decode_rows(weight_codes, column_scale):
    sign_bit = (weight_codes // 128).astype(jnp.float32)
    exponent_field = (weight_codes // 8 % 16).astype(jnp.float32)
    mantissa = (weight_codes % 8).astype(jnp.float32)
    magnitude = jnp.exp2(exponent_field - 7.0) * (1.0 + mantissa / 8.0)
    return ((1.0 - 2.0 * sign_bit) * magnitude * column_scale).astype(jnp.bfloat16)


def attention_kernel(
    core_ref,
    q_own,
    g_own,
    q_other,
    g_other,
    kv_own,
    kv_halo,
    key_mark,
    query_mark,
    dq_own,
    dq_other,
    dkv_halo,
    dkv_own,
    ka,
    kt,
    va,
    qa,
    ga,
    s_scr,
    d_scr,
    p_scr,
    ds_scr,
    dk_acc,
    dv_acc,
):
    slot = pl.program_id(0)
    step = pl.program_id(1)
    steps = pl.num_programs(1)
    rows = HEADS_STEP * HEAD_WIDTH
    blocks = DOC_LIMIT // 128 + 1

    @pl.when((slot == 0) & (step == 0))
    def _():
        ka[:, 128:] = key_mark[...]
        for i in range(DOC_LIMIT // 256 + 1):
            block = kv_halo[i] if i < DOC_LIMIT // 256 else kv_own[...]
            at = slice(i * 256, (i + 1) * 256)
            ka[at, :128] = block[:, :128]
            va[at, :] = block[:, 128:]
            kt[:, at] = block[:, :128].T
        dk_acc[...] = jnp.zeros_like(dk_acc)
        dv_acc[...] = jnp.zeros_like(dv_acc)

    @pl.when(step == 0)
    def _():
        for h in range(HEADS_STEP):
            qa[h * 128 : (h + 1) * 128, 128:] = query_mark[0]

    @pl.when(slot == 0)
    def _():
        for h in range(HEADS_STEP):
            qa[h * 128 : (h + 1) * 128, :128] = q_own[:, h * 128 : (h + 1) * 128]
            ga[h * 128 : (h + 1) * 128, :] = g_own[:, h * 128 : (h + 1) * 128]

    @pl.when(slot == 1)
    def _():
        for h in range(HEADS_STEP):
            qa[h * 128 : (h + 1) * 128, :128] = q_other[:, h * 128 : (h + 1) * 128]
            ga[h * 128 : (h + 1) * 128, :] = g_other[:, h * 128 : (h + 1) * 128]

    half = (core_ref[0] + slot) % 2
    first = pl.multiple_of(half * 128, 128)
    q_all = qa[...]
    g_all = ga[...]

    best = jnp.full((8, rows), masked_bias, jnp.float32)
    for b in range(blocks):
        at = pl.ds(pl.multiple_of(first + b * 128, 128), 128)
        s = dot(ka[at, :], q_all, NT)
        if b == blocks - 1:
            key_at = lax.broadcasted_iota(jnp.int32, (128, rows), 0)
            query_at = lax.broadcasted_iota(jnp.int32, (128, rows), 1) % 128
            s = jnp.where(key_at <= query_at, s, masked_bias)
        s_scr[b * 128 : (b + 1) * 128, :] = s
        best = jnp.maximum(best, jnp.max(s.reshape(16, 8, rows), axis=0))
        d_scr[b * 128 : (b + 1) * 128, :] = dot(va[at, :], g_all, NT)
    row_max = jnp.max(best, axis=0, keepdims=True) * exp2_scale
    total = jnp.zeros((8, rows), jnp.float32)
    for b in range(blocks):
        here = slice(b * 128, (b + 1) * 128)
        e = jnp.exp2(s_scr[here, :] * exp2_scale - row_max)
        s_scr[here, :] = e
        total = total + jnp.sum(e.reshape(16, 8, rows), axis=0)
    inverse = 1.0 / jnp.sum(total, axis=0, keepdims=True)
    delta = jnp.zeros((8, rows), jnp.float32)
    for b in range(blocks):
        here = slice(b * 128, (b + 1) * 128)
        p = s_scr[here, :] * inverse
        s_scr[here, :] = p
        p_bf = p.astype(jnp.bfloat16)
        p_scr[here, :] = p_bf
        term = p_bf.astype(jnp.float32) * d_scr[here, :]
        delta = delta + jnp.sum(term.reshape(16, 8, rows), axis=0)
    row_delta = jnp.sum(delta, axis=0, keepdims=True)
    for b in range(blocks):
        here = slice(b * 128, (b + 1) * 128)
        ds_scr[here, :] = (s_scr[here, :] * (d_scr[here, :] - row_delta)).astype(jnp.bfloat16)
    window = pl.ds(first, blocks * 128)
    dv_acc[window, :] += dot(p_scr[...], g_all, NN)
    dk_acc[window, :] += dot(ds_scr[...], q_all[:, :128], NN)
    dq_t = dot(kt[:, window], ds_scr[...], NN) * score_scale

    @pl.when(slot == 0)
    def _():
        for h in range(HEADS_STEP):
            at = slice(h * 128, (h + 1) * 128)
            dq_own[:, at] = dq_t[:, at].T.astype(jnp.bfloat16)

    @pl.when(slot == 1)
    def _():
        for h in range(HEADS_STEP):
            at = slice(h * 128, (h + 1) * 128)
            dq_other[:, at] = dq_t[:, at].T.astype(jnp.bfloat16)

    @pl.when((slot == 1) & (step == steps - 1))
    def _():
        for i in range(DOC_LIMIT // 256):
            at = slice(i * 256, (i + 1) * 256)
            dkv_halo[i, :, :128] = (dk_acc[at, :] * score_scale).astype(jnp.bfloat16)
            dkv_halo[i, :, 128:] = dv_acc[at, :].astype(jnp.bfloat16)
        dkv_own[:, :128] = dk_acc[DOC_LIMIT:, :] * score_scale
        dkv_own[:, 128:] = dv_acc[DOC_LIMIT:, :]


def attend_grads(core, queries, grads, q_other, g_other, kv_own, kv_halo, key_mark, query_mark):
    steps = GROUP_HEADS // HEADS_STEP
    width = HEADS_STEP * HEAD_WIDTH
    rows = width
    window = DOC_LIMIT + 256
    keys = DOC_LIMIT + 128
    bf16, f32 = jnp.bfloat16, jnp.float32

    def own_in(s, j, c):
        return (0, c[0] * steps + jnp.where(s == 0, j, steps - 1))

    def own_out(s, j, c):
        return (0, jnp.where(s == 0, j, steps - 1))

    def other(s, j, c):
        return (0, jnp.where(s == 0, 0, j))

    def fixed(rank):
        return lambda s, j, c: (0,) * rank

    return pl.pallas_call(
        attention_kernel,
        grid_spec=pltpu.PrefetchScalarGridSpec(
            num_scalar_prefetch=1,
            grid=(2, steps),
            in_specs=[
                pl.BlockSpec((128, width), own_in),
                pl.BlockSpec((128, width), own_in),
                pl.BlockSpec((128, width), other),
                pl.BlockSpec((128, width), other),
                pl.BlockSpec((256, 256), fixed(2)),
                pl.BlockSpec((DOC_LIMIT // 256, 256, 256), fixed(3)),
                pl.BlockSpec((window, 128), fixed(2)),
                pl.BlockSpec((1, 128, 128), lambda s, j, c: (s, 0, 0)),
            ],
            out_specs=[
                pl.BlockSpec((128, width), own_out),
                pl.BlockSpec((128, width), other),
                pl.BlockSpec((DOC_LIMIT // 256, 256, 256), fixed(3)),
                pl.BlockSpec((256, 256), fixed(2)),
            ],
            scratch_shapes=[
                pltpu.VMEM((window, 256), bf16),
                pltpu.VMEM((128, window), bf16),
                pltpu.VMEM((window, 128), bf16),
                pltpu.VMEM((rows, 256), bf16),
                pltpu.VMEM((rows, 128), bf16),
                pltpu.VMEM((keys, rows), f32),
                pltpu.VMEM((keys, rows), f32),
                pltpu.VMEM((keys, rows), bf16),
                pltpu.VMEM((keys, rows), bf16),
                pltpu.VMEM((window, 128), f32),
                pltpu.VMEM((window, 128), f32),
            ],
        ),
        out_shape=[
            jax.ShapeDtypeStruct((128, GROUP_COLS), bf16),
            jax.ShapeDtypeStruct((128, GROUP_COLS), bf16),
            jax.ShapeDtypeStruct((DOC_LIMIT // 256, 256, 256), bf16),
            jax.ShapeDtypeStruct((256, 256), f32),
        ],
        compiler_params=pltpu.CompilerParams(
            dimension_semantics=("arbitrary", "arbitrary"), vmem_limit_bytes=40 * 1024 * 1024
        ),
        cost_estimate=pl.CostEstimate(
            flops=12 * 2 * 16 * 128 * keys * 128,
            bytes_accessed=5 << 20,
            transcendentals=32 * 128 * keys,
        ),
    )(core, queries, grads, q_other, g_other, kv_own, kv_halo, key_mark, query_mark)


def on_device(
    activations,
    queries,
    saved_keys,
    saved_values,
    output_gradient,
    segments,
    weight_codes,
    exponents,
):
    bf16, f32 = jnp.bfloat16, jnp.float32
    dp_size, seq_size = lax.axis_size("dp"), lax.axis_size("seq")
    dp_idx, seq_idx = lax.axis_index("dp"), lax.axis_index("seq")
    core = seq_idx % 2
    chip = seq_idx // 2
    chips = seq_size // 2
    same_core = [[2 * k + c for k in range(chips)] for c in range(2)]
    swap_cores = [(i, i ^ 1) for i in range(seq_size)]
    halo_chips = DOC_LIMIT // 256

    def head_cols(array, which, width):
        return lax.dynamic_slice_in_dim(array, which * width, width, 1)

    kv_mine = jnp.concatenate(
        [head_cols(saved_keys, core, 128), head_cols(saved_values, core, 128)], axis=1
    )
    kv_theirs = jnp.concatenate(
        [head_cols(saved_keys, 1 - core, 128), head_cols(saved_values, 1 - core, 128)], axis=1
    )
    kv_got = lax.ppermute(kv_theirs, "seq", swap_cores)
    kv_own = jnp.where(
        core == 0,
        jnp.concatenate([kv_mine, kv_got], axis=0),
        jnp.concatenate([kv_got, kv_mine], axis=0),
    )
    kv_halo = jnp.stack(
        [
            lax.ppermute(kv_own, "seq", [(i, i + 2 * d) for i in range(seq_size - 2 * d)])
            for d in range(halo_chips, 0, -1)
        ]
    )
    q_other = lax.ppermute(head_cols(queries, 1 - core, GROUP_COLS), "seq", swap_cores)
    g_other = lax.ppermute(head_cols(output_gradient, 1 - core, GROUP_COLS), "seq", swap_cores)

    docs = segments[0]
    padded = jnp.concatenate([jnp.full((DOC_LIMIT,), 127, jnp.int32), docs])
    key_docs = lax.dynamic_slice_in_dim(padded, chip * 256, DOC_LIMIT + 256, 0)
    own_docs = lax.dynamic_slice_in_dim(docs, seq_idx * 128, 128, 0)
    other_docs = lax.dynamic_slice_in_dim(docs, (seq_idx + 1 - 2 * core) * 128, 128, 0)
    lanes = jnp.arange(128, dtype=jnp.int32)
    key_mark = (key_docs[:, None] == lanes[None, :]).astype(bf16)
    query_mark = jnp.where(
        jnp.stack([own_docs, other_docs])[:, :, None] == lanes[None, None, :], 0.0, masked_bias
    ).astype(bf16)

    rows_dev = weight_codes.shape[0]
    first_global = (dp_idx * seq_size + seq_idx) * rows_dev
    row_block = (first_global + jnp.arange(rows_dev)) // SCALE_BLOCK_SIDE
    row_pick = (row_block[:, None] == jnp.arange(exponents.shape[0])[None, :]).astype(f32)
    row_scale = jnp.dot(
        row_pick, jnp.exp2(exponents.astype(f32)), precision=lax.Precision.HIGHEST
    )
    column_scale = jnp.repeat(row_scale, SCALE_BLOCK_SIDE, axis=1)
    weight_rows = decode_rows(weight_codes, column_scale)
    crossed = lax.ppermute(
        weight_rows,
        ("dp", "seq"),
        [
            (a * seq_size + b, b * seq_size + a)
            for a in range(dp_size)
            for b in range(seq_size)
        ],
    )
    weight_block = lax.all_gather(crossed, "dp", axis=0, tiled=True)

    tokens = activations.shape[0]
    piece = activations.shape[1] // (dp_size * seq_size)
    act_rows = (
        activations.T.reshape(dp_size, seq_size, piece, tokens)
        .transpose(1, 0, 2, 3)
        .reshape(seq_size, dp_size * piece, tokens)
    )
    act_rows, _ = lax.optimization_barrier((act_rows, kv_halo))
    act_all = lax.all_to_all(act_rows, "seq", split_axis=0, concat_axis=0)
    act_all = act_all.transpose(1, 0, 2).reshape(dp_size * piece, seq_size * tokens)

    dq_own, dq_other, dkv_halo, dkv_own = attend_grads(
        core.reshape(1), queries, output_gradient, q_other, g_other, kv_own, kv_halo,
        key_mark, query_mark,
    )
    dq_back = lax.ppermute(dq_other, "seq", swap_cores)
    grad_q = jnp.where(
        core == 0,
        jnp.concatenate([dq_own, dq_back], axis=1),
        jnp.concatenate([dq_back, dq_own], axis=1),
    )

    kv_sum = dkv_own
    for d in range(1, halo_chips + 1):
        part = lax.ppermute(
            dkv_halo[halo_chips - d], "seq", [(i, i - 2 * d) for i in range(2 * d, seq_size)]
        )
        kv_sum = kv_sum + part.astype(f32)
    kv_chip = kv_sum.astype(bf16)
    kv_group = lax.all_to_all(
        jnp.broadcast_to(kv_chip[None], (chips,) + kv_chip.shape),
        "seq",
        split_axis=0,
        concat_axis=0,
        axis_index_groups=same_core,
    ).reshape(chips * 256, 256)
    kv_swap = lax.ppermute(kv_group, "seq", swap_cores)
    low = jnp.where(core == 0, kv_group, kv_swap)
    high = jnp.where(core == 0, kv_swap, kv_group)
    kv_grad = jnp.concatenate(
        [low[:, :128], high[:, :128], low[:, 128:], high[:, 128:]], axis=1
    )

    weight_part = dot(act_all, kv_grad, NN).astype(bf16)
    got = lax.all_to_all(
        weight_part.reshape(dp_size, piece, weight_part.shape[1]),
        "dp",
        split_axis=0,
        concat_axis=0,
    )
    grad_weights = jnp.sum(got.astype(f32), axis=0)
    grad_x_cols = dot(kv_grad, weight_block, NT).astype(bf16)
    grad_x = lax.all_to_all(grad_x_cols, "seq", split_axis=0, concat_axis=1, tiled=True)
    return (grad_q, grad_x, grad_weights)


def solution(mesh):
    return jax.shard_map(
        on_device,
        mesh=mesh,
        in_specs=(
            P(("dp", "seq"), None),
            P(("dp", "seq"), None),
            P(("dp", "seq"), None),
            P(("dp", "seq"), None),
            P(("dp", "seq"), None),
            P("dp", None),
            P(("dp", "seq"), None),
            P(),
        ),
        out_specs=(P(("dp", "seq"), None), P(("dp", "seq"), None), P(("dp", "seq"), None)),
        check_vma=False,
    )
```

```python
import math

import jax
import jax.numpy as jnp
from jax import lax
from jax.experimental import pallas as pl
from jax.experimental.pallas import tpu as pltpu
from jax.sharding import PartitionSpec as P

QUERY_HEADS = 32
KEY_VALUE_HEADS = 2
HEAD_WIDTH = 128
SCALE_BLOCK_SIDE = 128
GROUP_HEADS = QUERY_HEADS // KEY_VALUE_HEADS
GROUP_COLS = GROUP_HEADS * HEAD_WIDTH
DOC_LIMIT = 1024
HEADS_STEP = 4

masked_bias = -1e30
score_scale = 1.0 / math.sqrt(HEAD_WIDTH)
exp2_scale = score_scale * math.log2(math.e)

NT = (((1,), (1,)), ((), ()))
NN = (((1,), (0,)), ((), ()))


def dot(a, b, dims):
    return lax.dot_general(a, b, dims, preferred_element_type=jnp.float32)


def decode_rows(weight_codes, column_scale):
    sign_bit = (weight_codes // 128).astype(jnp.float32)
    exponent_field = (weight_codes // 8 % 16).astype(jnp.float32)
    mantissa = (weight_codes % 8).astype(jnp.float32)
    magnitude = jnp.exp2(exponent_field - 7.0) * (1.0 + mantissa / 8.0)
    return ((1.0 - 2.0 * sign_bit) * magnitude * column_scale).astype(jnp.bfloat16)


def attention_kernel(
    core_ref,
    q_own,
    g_own,
    q_other,
    g_other,
    kv_own,
    kv_halo,
    key_mark,
    query_mark,
    dq_own,
    dq_other,
    dkv_halo,
    dkv_own,
    ka,
    kt,
    va,
    qa,
    ga,
    s_scr,
    d_scr,
    p_scr,
    ds_scr,
    dk_acc,
    dv_acc,
):
    slot = pl.program_id(0)
    step = pl.program_id(1)
    steps = pl.num_programs(1)
    rows = HEADS_STEP * HEAD_WIDTH
    blocks = DOC_LIMIT // 128 + 1

    @pl.when((slot == 0) & (step == 0))
    def _():
        ka[:, 128:] = key_mark[...]
        for i in range(DOC_LIMIT // 256 + 1):
            block = kv_halo[i] if i < DOC_LIMIT // 256 else kv_own[...]
            at = slice(i * 256, (i + 1) * 256)
            ka[at, :128] = block[:, :128]
            va[at, :] = block[:, 128:]
            kt[:, at] = block[:, :128].T
        dk_acc[...] = jnp.zeros_like(dk_acc)
        dv_acc[...] = jnp.zeros_like(dv_acc)

    @pl.when(step == 0)
    def _():
        for h in range(HEADS_STEP):
            qa[h * 128 : (h + 1) * 128, 128:] = query_mark[0]

    @pl.when(slot == 0)
    def _():
        for h in range(HEADS_STEP):
            qa[h * 128 : (h + 1) * 128, :128] = q_own[:, h * 128 : (h + 1) * 128]
            ga[h * 128 : (h + 1) * 128, :] = g_own[:, h * 128 : (h + 1) * 128]

    @pl.when(slot == 1)
    def _():
        for h in range(HEADS_STEP):
            qa[h * 128 : (h + 1) * 128, :128] = q_other[:, h * 128 : (h + 1) * 128]
            ga[h * 128 : (h + 1) * 128, :] = g_other[:, h * 128 : (h + 1) * 128]

    half = (core_ref[0] + slot) % 2
    first = pl.multiple_of(half * 128, 128)
    q_all = qa[...]
    g_all = ga[...]

    best = jnp.full((8, rows), masked_bias, jnp.float32)
    for b in range(blocks):
        at = pl.ds(pl.multiple_of(first + b * 128, 128), 128)
        s = dot(ka[at, :], q_all, NT)
        if b == blocks - 1:
            key_at = lax.broadcasted_iota(jnp.int32, (128, rows), 0)
            query_at = lax.broadcasted_iota(jnp.int32, (128, rows), 1) % 128
            s = jnp.where(key_at <= query_at, s, masked_bias)
        s_scr[b * 128 : (b + 1) * 128, :] = s
        best = jnp.maximum(best, jnp.max(s.reshape(16, 8, rows), axis=0))
        d_scr[b * 128 : (b + 1) * 128, :] = dot(va[at, :], g_all, NT)
    row_max = jnp.max(best, axis=0, keepdims=True) * exp2_scale
    total = jnp.zeros((8, rows), jnp.float32)
    for b in range(blocks):
        here = slice(b * 128, (b + 1) * 128)
        e = jnp.exp2(s_scr[here, :] * exp2_scale - row_max)
        s_scr[here, :] = e
        total = total + jnp.sum(e.reshape(16, 8, rows), axis=0)
    inverse = 1.0 / jnp.sum(total, axis=0, keepdims=True)
    delta = jnp.zeros((8, rows), jnp.float32)
    for b in range(blocks):
        here = slice(b * 128, (b + 1) * 128)
        p = s_scr[here, :] * inverse
        s_scr[here, :] = p
        p_bf = p.astype(jnp.bfloat16)
        p_scr[here, :] = p_bf
        term = p_bf.astype(jnp.float32) * d_scr[here, :]
        delta = delta + jnp.sum(term.reshape(16, 8, rows), axis=0)
    row_delta = jnp.sum(delta, axis=0, keepdims=True)
    for b in range(blocks):
        here = slice(b * 128, (b + 1) * 128)
        ds_scr[here, :] = (s_scr[here, :] * (d_scr[here, :] - row_delta)).astype(jnp.bfloat16)
    window = pl.ds(first, blocks * 128)
    dv_acc[window, :] += dot(p_scr[...], g_all, NN)
    dk_acc[window, :] += dot(ds_scr[...], q_all[:, :128], NN)
    dq_t = dot(kt[:, window], ds_scr[...], NN) * score_scale

    @pl.when(slot == 0)
    def _():
        for h in range(HEADS_STEP):
            at = slice(h * 128, (h + 1) * 128)
            dq_own[:, at] = dq_t[:, at].T.astype(jnp.bfloat16)

    @pl.when(slot == 1)
    def _():
        for h in range(HEADS_STEP):
            at = slice(h * 128, (h + 1) * 128)
            dq_other[:, at] = dq_t[:, at].T.astype(jnp.bfloat16)

    @pl.when((slot == 1) & (step == steps - 1))
    def _():
        for i in range(DOC_LIMIT // 256):
            at = slice(i * 256, (i + 1) * 256)
            dkv_halo[i, :, :128] = (dk_acc[at, :] * score_scale).astype(jnp.bfloat16)
            dkv_halo[i, :, 128:] = dv_acc[at, :].astype(jnp.bfloat16)
        dkv_own[:, :128] = dk_acc[DOC_LIMIT:, :] * score_scale
        dkv_own[:, 128:] = dv_acc[DOC_LIMIT:, :]


def attend_grads(core, queries, grads, q_other, g_other, kv_own, kv_halo, key_mark, query_mark):
    steps = GROUP_HEADS // HEADS_STEP
    width = HEADS_STEP * HEAD_WIDTH
    rows = width
    window = DOC_LIMIT + 256
    keys = DOC_LIMIT + 128
    bf16, f32 = jnp.bfloat16, jnp.float32

    def own_in(s, j, c):
        return (0, c[0] * steps + jnp.where(s == 0, j, steps - 1))

    def own_out(s, j, c):
        return (0, jnp.where(s == 0, j, steps - 1))

    def other(s, j, c):
        return (0, jnp.where(s == 0, 0, j))

    def fixed(rank):
        return lambda s, j, c: (0,) * rank

    return pl.pallas_call(
        attention_kernel,
        grid_spec=pltpu.PrefetchScalarGridSpec(
            num_scalar_prefetch=1,
            grid=(2, steps),
            in_specs=[
                pl.BlockSpec((128, width), own_in),
                pl.BlockSpec((128, width), own_in),
                pl.BlockSpec((128, width), other),
                pl.BlockSpec((128, width), other),
                pl.BlockSpec((256, 256), fixed(2)),
                pl.BlockSpec((DOC_LIMIT // 256, 256, 256), fixed(3)),
                pl.BlockSpec((window, 128), fixed(2)),
                pl.BlockSpec((1, 128, 128), lambda s, j, c: (s, 0, 0)),
            ],
            out_specs=[
                pl.BlockSpec((128, width), own_out),
                pl.BlockSpec((128, width), other),
                pl.BlockSpec((DOC_LIMIT // 256, 256, 256), fixed(3)),
                pl.BlockSpec((256, 256), fixed(2)),
            ],
            scratch_shapes=[
                pltpu.VMEM((window, 256), bf16),
                pltpu.VMEM((128, window), bf16),
                pltpu.VMEM((window, 128), bf16),
                pltpu.VMEM((rows, 256), bf16),
                pltpu.VMEM((rows, 128), bf16),
                pltpu.VMEM((keys, rows), f32),
                pltpu.VMEM((keys, rows), f32),
                pltpu.VMEM((keys, rows), bf16),
                pltpu.VMEM((keys, rows), bf16),
                pltpu.VMEM((window, 128), f32),
                pltpu.VMEM((window, 128), f32),
            ],
        ),
        out_shape=[
            jax.ShapeDtypeStruct((128, GROUP_COLS), bf16),
            jax.ShapeDtypeStruct((128, GROUP_COLS), bf16),
            jax.ShapeDtypeStruct((DOC_LIMIT // 256, 256, 256), bf16),
            jax.ShapeDtypeStruct((256, 256), f32),
        ],
        compiler_params=pltpu.CompilerParams(
            dimension_semantics=("arbitrary", "arbitrary"), vmem_limit_bytes=40 * 1024 * 1024
        ),
        cost_estimate=pl.CostEstimate(
            flops=12 * 2 * 16 * 128 * keys * 128,
            bytes_accessed=5 << 20,
            transcendentals=32 * 128 * keys,
        ),
    )(core, queries, grads, q_other, g_other, kv_own, kv_halo, key_mark, query_mark)


def on_device(
    activations,
    queries,
    saved_keys,
    saved_values,
    output_gradient,
    segments,
    weight_codes,
    exponents,
):
    bf16, f32 = jnp.bfloat16, jnp.float32
    dp_size, seq_size = lax.axis_size("dp"), lax.axis_size("seq")
    dp_idx, seq_idx = lax.axis_index("dp"), lax.axis_index("seq")
    core = seq_idx % 2
    chip = seq_idx // 2
    chips = seq_size // 2
    same_core = [[2 * k + c for k in range(chips)] for c in range(2)]
    swap_cores = [(i, i ^ 1) for i in range(seq_size)]
    halo_chips = DOC_LIMIT // 256

    def head_cols(array, which, width):
        return lax.dynamic_slice_in_dim(array, which * width, width, 1)

    kv_mine = jnp.concatenate(
        [head_cols(saved_keys, core, 128), head_cols(saved_values, core, 128)], axis=1
    )
    kv_theirs = jnp.concatenate(
        [head_cols(saved_keys, 1 - core, 128), head_cols(saved_values, 1 - core, 128)], axis=1
    )
    kv_got = lax.ppermute(kv_theirs, "seq", swap_cores)
    kv_own = jnp.where(
        core == 0,
        jnp.concatenate([kv_mine, kv_got], axis=0),
        jnp.concatenate([kv_got, kv_mine], axis=0),
    )
    kv_halo = jnp.stack(
        [
            lax.ppermute(kv_own, "seq", [(i, i + 2 * d) for i in range(seq_size - 2 * d)])
            for d in range(halo_chips, 0, -1)
        ]
    )
    q_other = lax.ppermute(head_cols(queries, 1 - core, GROUP_COLS), "seq", swap_cores)
    g_other = lax.ppermute(head_cols(output_gradient, 1 - core, GROUP_COLS), "seq", swap_cores)

    docs = segments[0]
    padded = jnp.concatenate([jnp.full((DOC_LIMIT,), 127, jnp.int32), docs])
    key_docs = lax.dynamic_slice_in_dim(padded, chip * 256, DOC_LIMIT + 256, 0)
    own_docs = lax.dynamic_slice_in_dim(docs, seq_idx * 128, 128, 0)
    other_docs = lax.dynamic_slice_in_dim(docs, (seq_idx + 1 - 2 * core) * 128, 128, 0)
    lanes = jnp.arange(128, dtype=jnp.int32)
    key_mark = (key_docs[:, None] == lanes[None, :]).astype(bf16)
    query_mark = jnp.where(
        jnp.stack([own_docs, other_docs])[:, :, None] == lanes[None, None, :], 0.0, masked_bias
    ).astype(bf16)

    rows_dev = weight_codes.shape[0]
    first_global = (dp_idx * seq_size + seq_idx) * rows_dev
    row_block = (first_global + jnp.arange(rows_dev)) // SCALE_BLOCK_SIDE
    row_pick = (row_block[:, None] == jnp.arange(exponents.shape[0])[None, :]).astype(f32)
    row_scale = jnp.dot(
        row_pick, jnp.exp2(exponents.astype(f32)), precision=lax.Precision.HIGHEST
    )
    column_scale = jnp.repeat(row_scale, SCALE_BLOCK_SIDE, axis=1)
    weight_rows = decode_rows(weight_codes, column_scale)
    crossed = lax.ppermute(
        weight_rows,
        ("dp", "seq"),
        [
            (a * seq_size + b, b * seq_size + a)
            for a in range(dp_size)
            for b in range(seq_size)
        ],
    )
    x_size = 4
    x_at, z_at = dp_idx % x_size, dp_idx // x_size
    z_size = dp_size // x_size

    def x_turn(d):
        return [
            (i, i // x_size * x_size + (i % x_size + d) % x_size) for i in range(dp_size)
        ]

    def z_turn(d):
        return [(i, (i // x_size + d) % z_size * x_size + i % x_size) for i in range(dp_size)]

    def ring_gather(block, turn, size, at):
        parts = [block] + [lax.ppermute(block, "dp", turn(d)) for d in range(1, size)]
        stacked = jnp.stack(parts[::-1] + parts[:0:-1])
        return lax.dynamic_slice_in_dim(stacked, size - 1 - at, size, 0)

    weight_row = ring_gather(crossed, x_turn, x_size, x_at)
    weight_block = ring_gather(weight_row, z_turn, z_size, z_at).reshape(
        dp_size * rows_dev, weight_rows.shape[1]
    )
    own_cols = jnp.concatenate(
        [head_cols(weight_block, core, 128), head_cols(weight_block, 2 + core, 128)], axis=1
    )
    other_cols = jnp.concatenate(
        [head_cols(weight_block, 1 - core, 128), head_cols(weight_block, 3 - core, 128)], axis=1
    )

    tokens = activations.shape[0]
    piece = activations.shape[1] // (dp_size * seq_size)
    act_rows = (
        activations.T.reshape(dp_size, seq_size, piece, tokens)
        .transpose(1, 0, 2, 3)
        .reshape(seq_size, dp_size * piece, tokens)
    )
    act_rows, _ = lax.optimization_barrier((act_rows, kv_halo))
    act_all = lax.all_to_all(act_rows, "seq", split_axis=0, concat_axis=0)
    act_all = act_all.transpose(1, 0, 2).reshape(dp_size * piece, seq_size * tokens)

    dq_own, dq_other, dkv_halo, dkv_own = attend_grads(
        core.reshape(1), queries, output_gradient, q_other, g_other, kv_own, kv_halo,
        key_mark, query_mark,
    )
    dq_back = lax.ppermute(dq_other, "seq", swap_cores)
    grad_q = jnp.where(
        core == 0,
        jnp.concatenate([dq_own, dq_back], axis=1),
        jnp.concatenate([dq_back, dq_own], axis=1),
    )

    dkv_halo, dkv_own, act_all, own_cols, other_cols = lax.optimization_barrier(
        (dkv_halo, dkv_own, act_all, own_cols, other_cols)
    )
    kv_sum = dkv_own
    for d in range(1, halo_chips + 1):
        part = lax.ppermute(
            dkv_halo[halo_chips - d], "seq", [(i, i - 2 * d) for i in range(2 * d, seq_size)]
        )
        kv_sum = kv_sum + part.astype(f32)
    kv_chip = kv_sum.astype(bf16)
    kv_group = lax.all_to_all(
        jnp.broadcast_to(kv_chip[None], (chips,) + kv_chip.shape),
        "seq",
        split_axis=0,
        concat_axis=0,
        axis_index_groups=same_core,
    ).reshape(chips * 256, 256)
    kv_swap = lax.ppermute(kv_group, "seq", swap_cores)
    grad_x_cols = (dot(kv_group, own_cols, NT) + dot(kv_swap, other_cols, NT)).astype(bf16)
    weight_part = jnp.concatenate(
        [dot(act_all, kv_group, NN), dot(act_all, kv_swap, NN)], axis=1
    ).astype(bf16)

    def ring_scatter(blocks, turn, size, at):
        total = lax.dynamic_index_in_dim(blocks, at, 0, keepdims=False).astype(f32)
        for d in range(1, size):
            block = lax.dynamic_index_in_dim(blocks, (at + d) % size, 0, keepdims=False)
            total = total + lax.ppermute(block.astype(bf16), "dp", turn(d)).astype(f32)
        return total

    blocks = weight_part.reshape(z_size, x_size, piece, weight_part.shape[1]).transpose(1, 0, 2, 3)
    in_row = ring_scatter(blocks, x_turn, x_size, x_at)
    total = ring_scatter(in_row, z_turn, z_size, z_at)
    own_k, own_v, other_k, other_v = (total[:, i * 128 : (i + 1) * 128] for i in range(4))
    grad_weights = jnp.where(
        core == 0,
        jnp.concatenate([own_k, other_k, own_v, other_v], axis=1),
        jnp.concatenate([other_k, own_k, other_v, own_v], axis=1),
    )
    grad_x = lax.all_to_all(grad_x_cols, "seq", split_axis=0, concat_axis=1, tiled=True)
    return (grad_q, grad_x, grad_weights)


def solution(mesh):
    return jax.shard_map(
        on_device,
        mesh=mesh,
        in_specs=(
            P(("dp", "seq"), None),
            P(("dp", "seq"), None),
            P(("dp", "seq"), None),
            P(("dp", "seq"), None),
            P(("dp", "seq"), None),
            P("dp", None),
            P(("dp", "seq"), None),
            P(),
        ),
        out_specs=(P(("dp", "seq"), None), P(("dp", "seq"), None), P(("dp", "seq"), None)),
        check_vma=False,
    )
```

```python
import math

import jax
import jax.numpy as jnp
from jax import lax
from jax.experimental import pallas as pl
from jax.experimental.pallas import tpu as pltpu
from jax.sharding import PartitionSpec as P

QUERY_HEADS = 32
KEY_VALUE_HEADS = 2
HEAD_WIDTH = 128
SCALE_BLOCK_SIDE = 128
GROUP_HEADS = QUERY_HEADS // KEY_VALUE_HEADS
GROUP_COLS = GROUP_HEADS * HEAD_WIDTH
DOC_LIMIT = 1024
HEADS_STEP = 8
WIDEN = 4
ROW_TILE = 256

masked_bias = -1e30
score_scale = 1.0 / math.sqrt(HEAD_WIDTH)
exp2_scale = score_scale * math.log2(math.e)

NT = (((1,), (1,)), ((), ()))
NN = (((1,), (0,)), ((), ()))


def dot(a, b, dims):
    return lax.dot_general(a, b, dims, preferred_element_type=jnp.float32)


def decode_rows(weight_codes, column_scale):
    sign_bit = (weight_codes // 128).astype(jnp.float32)
    exponent_field = (weight_codes // 8 % 16).astype(jnp.float32)
    mantissa = (weight_codes % 8).astype(jnp.float32)
    magnitude = jnp.exp2(exponent_field - 7.0) * (1.0 + mantissa / 8.0)
    return ((1.0 - 2.0 * sign_bit) * magnitude * column_scale).astype(jnp.bfloat16)


def attention_kernel(
    core_ref,
    q_own,
    g_own,
    q_other,
    g_other,
    kv_own,
    kv_1,
    kv_2,
    kv_3,
    kv_4,
    key_mark,
    query_mark,
    dq_own,
    dq_other,
    dkv_1,
    dkv_2,
    dkv_3,
    dkv_4,
    dkv_own,
    ka,
    kt,
    va,
    qa,
    ga,
    s_scr,
    d_scr,
    p_scr,
    ds_scr,
    dk_acc,
    dv_acc,
):
    slot = pl.program_id(0)
    step = pl.program_id(1)
    steps = pl.num_programs(1)
    rows = HEADS_STEP * HEAD_WIDTH
    blocks = DOC_LIMIT // 128 + 1

    @pl.when((slot == 0) & (step == 0))
    def _():
        ka[:, 128:] = key_mark[...]
        for i, block in enumerate((kv_4, kv_3, kv_2, kv_1, kv_own)):
            at = slice(i * 256, (i + 1) * 256)
            ka[at, :128] = block[:, :128]
            va[at, :] = block[:, 128:]
            kt[:, at] = block[:, :128].T
        dk_acc[...] = jnp.zeros_like(dk_acc)
        dv_acc[...] = jnp.zeros_like(dv_acc)

    @pl.when(step == 0)
    def _():
        for h in range(HEADS_STEP):
            qa[h * 128 : (h + 1) * 128, 128:] = query_mark[0]

    @pl.when(slot == 0)
    def _():
        for h in range(HEADS_STEP):
            qa[h * 128 : (h + 1) * 128, :128] = q_own[:, h * 128 : (h + 1) * 128]
            ga[h * 128 : (h + 1) * 128, :] = g_own[:, h * 128 : (h + 1) * 128]

    @pl.when(slot == 1)
    def _():
        for h in range(HEADS_STEP):
            qa[h * 128 : (h + 1) * 128, :128] = q_other[:, h * 128 : (h + 1) * 128]
            ga[h * 128 : (h + 1) * 128, :] = g_other[:, h * 128 : (h + 1) * 128]

    half = (core_ref[0] + slot) % 2
    first = pl.multiple_of(half * 128, 128)
    for t in range(rows // ROW_TILE):
        lanes = slice(t * ROW_TILE, (t + 1) * ROW_TILE)
        q_tile = qa[lanes, :]
        g_tile = ga[lanes, :]
        tops, sums, deltas = [], [], []
        for b in range(blocks):
            here = slice(b * 128, (b + 1) * 128)
            at = pl.ds(pl.multiple_of(first + b * 128, 128), 128)
            s = dot(ka[at, :], q_tile, NT)
            if b == blocks - 1:
                key_at = lax.broadcasted_iota(jnp.int32, (128, ROW_TILE), 0)
                query_at = lax.broadcasted_iota(jnp.int32, (128, ROW_TILE), 1) % 128
                s = jnp.where(key_at <= query_at, s, masked_bias)
            top = jnp.max(s, axis=0, keepdims=True)
            e = jnp.exp2((s - top) * exp2_scale)
            d = dot(va[at, :], g_tile, NT)
            s_scr[here, lanes] = e
            d_scr[here, lanes] = d
            tops.append(top)
            sums.append(jnp.sum(e, axis=0, keepdims=True))
            deltas.append(jnp.sum(e * d, axis=0, keepdims=True))
        best = tops[0]
        for b in range(1, blocks):
            best = jnp.maximum(best, tops[b])
        factors = [jnp.exp2((top - best) * exp2_scale) for top in tops]
        inverse = 1.0 / sum(f * x for f, x in zip(factors, sums))
        row_delta = sum(f * x for f, x in zip(factors, deltas)) * inverse
        for b in range(blocks):
            here = slice(b * 128, (b + 1) * 128)
            p = s_scr[here, lanes] * (factors[b] * inverse)
            p_scr[here, lanes] = p.astype(jnp.bfloat16)
            ds_scr[here, lanes] = (p * (d_scr[here, lanes] - row_delta)).astype(jnp.bfloat16)
    window = pl.ds(first, blocks * 128)
    dv_acc[window, :] += dot(p_scr[...], ga[...], NN)
    dk_acc[window, :] += dot(ds_scr[...], qa[:, :128], NN)
    dq_t = dot(kt[:, window], ds_scr[...], NN) * score_scale

    @pl.when(slot == 0)
    def _():
        for h in range(HEADS_STEP):
            at = slice(h * 128, (h + 1) * 128)
            dq_own[:, at] = dq_t[:, at].T.astype(jnp.bfloat16)

    @pl.when(slot == 1)
    def _():
        for h in range(HEADS_STEP):
            at = slice(h * 128, (h + 1) * 128)
            dq_other[:, at] = dq_t[:, at].T.astype(jnp.bfloat16)

    @pl.when((slot == 1) & (step == steps - 1))
    def _():
        for i, block in enumerate((dkv_4, dkv_3, dkv_2, dkv_1)):
            at = slice(i * 256, (i + 1) * 256)
            block[:, :128] = (dk_acc[at, :] * score_scale).astype(jnp.bfloat16)
            block[:, 128:] = dv_acc[at, :].astype(jnp.bfloat16)
        dkv_own[:, :128] = dk_acc[DOC_LIMIT:, :] * score_scale
        dkv_own[:, 128:] = dv_acc[DOC_LIMIT:, :]


def attend_grads(core, queries, grads, q_other, g_other, kv_own, kv_halo, key_mark, query_mark):
    steps = GROUP_HEADS // HEADS_STEP
    width = HEADS_STEP * HEAD_WIDTH
    rows = width
    window = DOC_LIMIT + 256
    keys = DOC_LIMIT + 128
    bf16, f32 = jnp.bfloat16, jnp.float32

    def own_in(s, j, c):
        return (0, c[0] * steps + jnp.where(s == 0, j, steps - 1))

    def own_out(s, j, c):
        return (0, jnp.where(s == 0, j, steps - 1))

    def other(s, j, c):
        return (0, jnp.where(s == 0, 0, j))

    def fixed(rank):
        return lambda s, j, c: (0,) * rank

    return pl.pallas_call(
        attention_kernel,
        grid_spec=pltpu.PrefetchScalarGridSpec(
            num_scalar_prefetch=1,
            grid=(2, steps),
            in_specs=[
                pl.BlockSpec((128, width), own_in),
                pl.BlockSpec((128, width), own_in),
                pl.BlockSpec((128, width), other),
                pl.BlockSpec((128, width), other),
                pl.BlockSpec((256, 256), fixed(2)),
                pl.BlockSpec((256, 256), fixed(2)),
                pl.BlockSpec((256, 256), fixed(2)),
                pl.BlockSpec((256, 256), fixed(2)),
                pl.BlockSpec((256, 256), fixed(2)),
                pl.BlockSpec((window, 128), fixed(2)),
                pl.BlockSpec((1, 128, 128), lambda s, j, c: (s, 0, 0)),
            ],
            out_specs=[
                pl.BlockSpec((128, width), own_out),
                pl.BlockSpec((128, width), other),
                pl.BlockSpec((256, 256), fixed(2)),
                pl.BlockSpec((256, 256), fixed(2)),
                pl.BlockSpec((256, 256), fixed(2)),
                pl.BlockSpec((256, 256), fixed(2)),
                pl.BlockSpec((256, 256), fixed(2)),
            ],
            scratch_shapes=[
                pltpu.VMEM((window, 256), bf16),
                pltpu.VMEM((128, window), bf16),
                pltpu.VMEM((window, 128), bf16),
                pltpu.VMEM((rows, 256), bf16),
                pltpu.VMEM((rows, 128), bf16),
                pltpu.VMEM((keys, rows), f32),
                pltpu.VMEM((keys, rows), f32),
                pltpu.VMEM((keys, rows), bf16),
                pltpu.VMEM((keys, rows), bf16),
                pltpu.VMEM((window, 128), f32),
                pltpu.VMEM((window, 128), f32),
            ],
        ),
        out_shape=[
            jax.ShapeDtypeStruct((128, GROUP_COLS), bf16),
            jax.ShapeDtypeStruct((128, GROUP_COLS), bf16),
            jax.ShapeDtypeStruct((256, 256), bf16),
            jax.ShapeDtypeStruct((256, 256), bf16),
            jax.ShapeDtypeStruct((256, 256), bf16),
            jax.ShapeDtypeStruct((256, 256), bf16),
            jax.ShapeDtypeStruct((256, 256), f32),
        ],
        compiler_params=pltpu.CompilerParams(
            dimension_semantics=("arbitrary", "arbitrary"), vmem_limit_bytes=56 * 1024 * 1024
        ),
        cost_estimate=pl.CostEstimate(
            flops=12 * 2 * 16 * 128 * keys * 128,
            bytes_accessed=5 << 20,
            transcendentals=32 * 128 * keys,
        ),
    )(core, queries, grads, q_other, g_other, kv_own, *kv_halo, key_mark, query_mark)


def on_device(
    activations,
    queries,
    saved_keys,
    saved_values,
    output_gradient,
    segments,
    weight_codes,
    exponents,
):
    bf16, f32 = jnp.bfloat16, jnp.float32
    dp_size, seq_size = lax.axis_size("dp"), lax.axis_size("seq")
    dp_idx, seq_idx = lax.axis_index("dp"), lax.axis_index("seq")
    core = seq_idx % 2
    chip = seq_idx // 2
    chips = seq_size // 2
    same_core = [[2 * k + c for k in range(chips)] for c in range(2)]
    swap_cores = [(i, i ^ 1) for i in range(seq_size)]
    halo_chips = DOC_LIMIT // 256

    def head_cols(array, which, width):
        return lax.dynamic_slice_in_dim(array, which * width, width, 1)

    kv_mine = jnp.concatenate(
        [head_cols(saved_keys, core, 128), head_cols(saved_values, core, 128)], axis=1
    )
    kv_theirs = jnp.concatenate(
        [head_cols(saved_keys, 1 - core, 128), head_cols(saved_values, 1 - core, 128)], axis=1
    )
    kv_got = lax.ppermute(kv_theirs, "seq", swap_cores)
    kv_own = jnp.where(
        core == 0,
        jnp.concatenate([kv_mine, kv_got], axis=0),
        jnp.concatenate([kv_got, kv_mine], axis=0),
    )
    kv_halo = [
        lax.ppermute(kv_own, "seq", [(i, i + 2 * d) for i in range(seq_size - 2 * d)])
        for d in range(1, halo_chips + 1)
    ]
    q_other = lax.ppermute(head_cols(queries, 1 - core, GROUP_COLS), "seq", swap_cores)
    g_other = lax.ppermute(head_cols(output_gradient, 1 - core, GROUP_COLS), "seq", swap_cores)

    docs = segments[0]
    padded = jnp.concatenate([jnp.full((DOC_LIMIT,), 127, jnp.int32), docs])
    key_docs = lax.dynamic_slice_in_dim(padded, chip * 256, DOC_LIMIT + 256, 0)
    own_docs = lax.dynamic_slice_in_dim(docs, seq_idx * 128, 128, 0)
    other_docs = lax.dynamic_slice_in_dim(docs, (seq_idx + 1 - 2 * core) * 128, 128, 0)
    lanes = jnp.arange(128, dtype=jnp.int32)
    key_mark = (key_docs[:, None] == lanes[None, :]).astype(bf16)
    query_mark = jnp.where(
        jnp.stack([own_docs, other_docs])[:, :, None] == lanes[None, None, :], 0.0, masked_bias
    ).astype(bf16)

    rows_dev = weight_codes.shape[0]
    first_global = (dp_idx * seq_size + seq_idx) * rows_dev
    row_block = (first_global + jnp.arange(rows_dev)) // SCALE_BLOCK_SIDE
    row_pick = (row_block[:, None] == jnp.arange(exponents.shape[0])[None, :]).astype(f32)
    row_scale = jnp.dot(
        row_pick, jnp.exp2(exponents.astype(f32)), precision=lax.Precision.HIGHEST
    )
    column_scale = jnp.repeat(row_scale, SCALE_BLOCK_SIDE, axis=1)
    weight_rows = decode_rows(weight_codes, column_scale)
    x_size = 4
    x_at, z_at = dp_idx % x_size, dp_idx // x_size
    z_size = dp_size // x_size

    def x_turn(d):
        return [
            (i, i // x_size * x_size + (i % x_size + d) % x_size) for i in range(dp_size)
        ]

    def z_turn(d):
        return [(i, (i // x_size + d) % z_size * x_size + i % x_size) for i in range(dp_size)]

    weight_block = (
        lax.all_gather(jnp.tile(weight_rows, (WIDEN, 1)), "dp", axis=0, tiled=True)
        .reshape(dp_size, WIDEN, rows_dev, weight_rows.shape[1])[:, 0]
        .reshape(dp_size * rows_dev, weight_rows.shape[1])
    )

    tokens = activations.shape[0]
    piece = activations.shape[1] // (dp_size * seq_size)
    act_rows = (
        activations.T.reshape(dp_size, seq_size, piece, tokens)
        .transpose(1, 0, 2, 3)
        .reshape(seq_size, dp_size * piece, tokens)
    )
    act_rows, *kv_halo = lax.optimization_barrier((act_rows, *kv_halo))
    arrived = lax.all_to_all(act_rows, "seq", split_axis=0, concat_axis=0)

    dq_own, dq_other, *dkv_halo, dkv_own = attend_grads(
        core.reshape(1), queries, output_gradient, q_other, g_other, kv_own, kv_halo,
        key_mark, query_mark,
    )
    dq_back = lax.ppermute(dq_other, "seq", swap_cores)
    grad_q = jnp.where(
        core == 0,
        jnp.concatenate([dq_own, dq_back], axis=1),
        jnp.concatenate([dq_back, dq_own], axis=1),
    )

    arrived_now, dkv_own, *dkv_halo = lax.optimization_barrier((arrived, dkv_own, *dkv_halo))
    act_all = arrived_now.transpose(1, 0, 2).reshape(dp_size * piece, seq_size * tokens)
    kv_sum = dkv_own
    for d in range(1, halo_chips + 1):
        part = lax.ppermute(
            dkv_halo[d - 1], "seq", [(i, i - 2 * d) for i in range(2 * d, seq_size)]
        )
        kv_sum = kv_sum + part.astype(f32)
    kv_chip, weight_block = lax.optimization_barrier((kv_sum.astype(bf16), weight_block))
    kv_group = lax.all_to_all(
        jnp.broadcast_to(kv_chip[None], (chips,) + kv_chip.shape),
        "seq",
        split_axis=0,
        concat_axis=0,
        axis_index_groups=same_core,
    ).reshape(chips * 256, 256)
    kv_swap = lax.ppermute(kv_group, "seq", swap_cores)
    weight_part = jnp.concatenate(
        [dot(act_all, kv_group, NN), dot(act_all, kv_swap, NN)], axis=1
    ).astype(bf16)

    def ring_scatter(blocks, turn, size, at):
        total = lax.dynamic_index_in_dim(blocks, at, 0, keepdims=False).astype(f32)
        for d in range(1, size):
            block = lax.dynamic_index_in_dim(blocks, (at + d) % size, 0, keepdims=False)
            total = total + lax.ppermute(block.astype(bf16), "dp", turn(d)).astype(f32)
        return total

    blocks = weight_part.reshape(z_size, x_size, piece, weight_part.shape[1]).transpose(1, 0, 2, 3)
    in_row = ring_scatter(blocks, x_turn, x_size, x_at)
    total = ring_scatter(in_row, z_turn, z_size, z_at)
    own_k, own_v, other_k, other_v = (total[:, i * 128 : (i + 1) * 128] for i in range(4))
    grad_weights = jnp.where(
        core == 0,
        jnp.concatenate([own_k, other_k, own_v, other_v], axis=1),
        jnp.concatenate([other_k, own_k, other_v, own_v], axis=1),
    )
    def cols_of(which):
        return jnp.concatenate(
            [head_cols(weight_block, which, 128), head_cols(weight_block, 2 + which, 128)], axis=1
        )

    grad_x_rows = (
        dot(cols_of(core), kv_group, NT) + dot(cols_of(1 - core), kv_swap, NT)
    ).astype(bf16)
    grad_x_rows = grad_x_rows.reshape(dp_size * piece, seq_size, tokens).transpose(1, 0, 2)
    grad_x = lax.all_to_all(grad_x_rows, "seq", split_axis=0, concat_axis=0)
    grad_x = (
        grad_x.reshape(seq_size, dp_size, piece, tokens)
        .transpose(1, 0, 2, 3)
        .reshape(dp_size * seq_size * piece, tokens)
        .T
    )
    return (grad_q, grad_x, grad_weights)


def solution(mesh):
    return jax.shard_map(
        on_device,
        mesh=mesh,
        in_specs=(
            P(("dp", "seq"), None),
            P(("dp", "seq"), None),
            P(("dp", "seq"), None),
            P(("dp", "seq"), None),
            P(("dp", "seq"), None),
            P("dp", None),
            P(("dp", "seq"), None),
            P(),
        ),
        out_specs=(P(("dp", "seq"), None), P(("dp", "seq"), None), P(("dp", "seq"), None)),
        check_vma=False,
    )
```

```python
import math

import jax
import jax.numpy as jnp
from jax import lax
from jax.experimental import pallas as pl
from jax.experimental.pallas import tpu as pltpu
from jax.sharding import PartitionSpec as P

QUERY_HEADS = 32
KEY_VALUE_HEADS = 2
HEAD_WIDTH = 128
SCALE_BLOCK_SIDE = 128
GROUP_HEADS = QUERY_HEADS // KEY_VALUE_HEADS
GROUP_COLS = GROUP_HEADS * HEAD_WIDTH
DOC_LIMIT = 1024
HEADS_STEP = 16
WIDEN = 4
ROW_TILE = 256

masked_bias = -1e30
score_scale = 1.0 / math.sqrt(HEAD_WIDTH)
exp2_scale = score_scale * math.log2(math.e)

NT = (((1,), (1,)), ((), ()))
NN = (((1,), (0,)), ((), ()))


def dot(a, b, dims):
    return lax.dot_general(a, b, dims, preferred_element_type=jnp.float32)


def decode_rows(weight_codes, column_scale):
    sign_bit = (weight_codes // 128).astype(jnp.float32)
    exponent_field = (weight_codes // 8 % 16).astype(jnp.float32)
    mantissa = (weight_codes % 8).astype(jnp.float32)
    magnitude = jnp.exp2(exponent_field - 7.0) * (1.0 + mantissa / 8.0)
    return ((1.0 - 2.0 * sign_bit) * magnitude * column_scale).astype(jnp.bfloat16)


def attention_kernel(
    core_ref,
    q_own,
    g_own,
    q_other,
    g_other,
    kv_own,
    kv_1,
    kv_2,
    kv_3,
    kv_4,
    key_mark,
    query_mark,
    dq_own,
    dq_other,
    dkv_1,
    dkv_2,
    dkv_3,
    dkv_4,
    dkv_own,
    ka,
    kt,
    va,
    qa,
    ga,
    s_scr,
    d_scr,
    p_scr,
    ds_scr,
    dk_acc,
    dv_acc,
):
    slot = pl.program_id(0)
    step = pl.program_id(1)
    steps = pl.num_programs(1)
    rows = HEADS_STEP * HEAD_WIDTH
    blocks = DOC_LIMIT // 128 + 1

    @pl.when((slot == 0) & (step == 0))
    def _():
        ka[:, 128:] = key_mark[...]
        for i, block in enumerate((kv_4, kv_3, kv_2, kv_1, kv_own)):
            at = slice(i * 256, (i + 1) * 256)
            ka[at, :128] = block[:, :128]
            va[at, :] = block[:, 128:]
            kt[:, at] = block[:, :128].T
        dk_acc[...] = jnp.zeros_like(dk_acc)
        dv_acc[...] = jnp.zeros_like(dv_acc)

    @pl.when(step == 0)
    def _():
        for h in range(HEADS_STEP):
            qa[h * 128 : (h + 1) * 128, 128:] = query_mark[0]

    @pl.when(slot == 0)
    def _():
        for h in range(HEADS_STEP):
            qa[h * 128 : (h + 1) * 128, :128] = q_own[:, h * 128 : (h + 1) * 128]
            ga[h * 128 : (h + 1) * 128, :] = g_own[:, h * 128 : (h + 1) * 128]

    @pl.when(slot == 1)
    def _():
        for h in range(HEADS_STEP):
            qa[h * 128 : (h + 1) * 128, :128] = q_other[:, h * 128 : (h + 1) * 128]
            ga[h * 128 : (h + 1) * 128, :] = g_other[:, h * 128 : (h + 1) * 128]

    half = (core_ref[0] + slot) % 2
    first = pl.multiple_of(half * 128, 128)
    for t in range(rows // ROW_TILE):
        lanes = slice(t * ROW_TILE, (t + 1) * ROW_TILE)
        q_tile = qa[lanes, :]
        g_tile = ga[lanes, :]
        tops, sums, deltas = [], [], []
        for b in range(blocks):
            here = slice(b * 128, (b + 1) * 128)
            at = pl.ds(pl.multiple_of(first + b * 128, 128), 128)
            s = dot(ka[at, :], q_tile, NT)
            if b == blocks - 1:
                key_at = lax.broadcasted_iota(jnp.int32, (128, ROW_TILE), 0)
                query_at = lax.broadcasted_iota(jnp.int32, (128, ROW_TILE), 1) % 128
                s = jnp.where(key_at <= query_at, s, masked_bias)
            top = jnp.max(s, axis=0, keepdims=True)
            e = jnp.exp2((s - top) * exp2_scale)
            d = dot(va[at, :], g_tile, NT)
            s_scr[here, lanes] = e
            d_scr[here, lanes] = d
            tops.append(top)
            sums.append(jnp.sum(e, axis=0, keepdims=True))
            deltas.append(jnp.sum(e * d, axis=0, keepdims=True))
        best = tops[0]
        for b in range(1, blocks):
            best = jnp.maximum(best, tops[b])
        factors = [jnp.exp2((top - best) * exp2_scale) for top in tops]
        inverse = 1.0 / sum(f * x for f, x in zip(factors, sums))
        row_delta = sum(f * x for f, x in zip(factors, deltas)) * inverse
        for b in range(blocks):
            here = slice(b * 128, (b + 1) * 128)
            p = s_scr[here, lanes] * (factors[b] * inverse)
            p_scr[here, lanes] = p.astype(jnp.bfloat16)
            ds_scr[here, lanes] = (p * (d_scr[here, lanes] - row_delta)).astype(jnp.bfloat16)
    window = pl.ds(first, blocks * 128)
    dv_acc[window, :] += dot(p_scr[...], ga[...], NN)
    dk_acc[window, :] += dot(ds_scr[...], qa[:, :128], NN)
    dq_t = dot(kt[:, window], ds_scr[...], NN) * score_scale

    @pl.when(slot == 0)
    def _():
        for h in range(HEADS_STEP):
            at = slice(h * 128, (h + 1) * 128)
            dq_own[:, at] = dq_t[:, at].T.astype(jnp.bfloat16)

    @pl.when(slot == 1)
    def _():
        for h in range(HEADS_STEP):
            at = slice(h * 128, (h + 1) * 128)
            dq_other[:, at] = dq_t[:, at].T.astype(jnp.bfloat16)

    @pl.when((slot == 1) & (step == steps - 1))
    def _():
        for i, block in enumerate((dkv_4, dkv_3, dkv_2, dkv_1)):
            at = slice(i * 256, (i + 1) * 256)
            block[:, :128] = (dk_acc[at, :] * score_scale).astype(jnp.bfloat16)
            block[:, 128:] = dv_acc[at, :].astype(jnp.bfloat16)
        dkv_own[:, :128] = dk_acc[DOC_LIMIT:, :] * score_scale
        dkv_own[:, 128:] = dv_acc[DOC_LIMIT:, :]


def attend_grads(core, queries, grads, q_other, g_other, kv_own, kv_halo, key_mark, query_mark):
    steps = GROUP_HEADS // HEADS_STEP
    width = HEADS_STEP * HEAD_WIDTH
    rows = width
    window = DOC_LIMIT + 256
    keys = DOC_LIMIT + 128
    bf16, f32 = jnp.bfloat16, jnp.float32

    def own_in(s, j, c):
        return (0, c[0] * steps + jnp.where(s == 0, j, steps - 1))

    def own_out(s, j, c):
        return (0, jnp.where(s == 0, j, steps - 1))

    def other(s, j, c):
        return (0, jnp.where(s == 0, 0, j))

    def fixed(rank):
        return lambda s, j, c: (0,) * rank

    return pl.pallas_call(
        attention_kernel,
        grid_spec=pltpu.PrefetchScalarGridSpec(
            num_scalar_prefetch=1,
            grid=(2, steps),
            in_specs=[
                pl.BlockSpec((128, width), own_in),
                pl.BlockSpec((128, width), own_in),
                pl.BlockSpec((128, width), other),
                pl.BlockSpec((128, width), other),
                pl.BlockSpec((256, 256), fixed(2)),
                pl.BlockSpec((256, 256), fixed(2)),
                pl.BlockSpec((256, 256), fixed(2)),
                pl.BlockSpec((256, 256), fixed(2)),
                pl.BlockSpec((256, 256), fixed(2)),
                pl.BlockSpec((window, 128), fixed(2)),
                pl.BlockSpec((1, 128, 128), lambda s, j, c: (s, 0, 0)),
            ],
            out_specs=[
                pl.BlockSpec((128, width), own_out),
                pl.BlockSpec((128, width), other),
                pl.BlockSpec((256, 256), fixed(2)),
                pl.BlockSpec((256, 256), fixed(2)),
                pl.BlockSpec((256, 256), fixed(2)),
                pl.BlockSpec((256, 256), fixed(2)),
                pl.BlockSpec((256, 256), fixed(2)),
            ],
            scratch_shapes=[
                pltpu.VMEM((window, 256), bf16),
                pltpu.VMEM((128, window), bf16),
                pltpu.VMEM((window, 128), bf16),
                pltpu.VMEM((rows, 256), bf16),
                pltpu.VMEM((rows, 128), bf16),
                pltpu.VMEM((keys, rows), f32),
                pltpu.VMEM((keys, rows), f32),
                pltpu.VMEM((keys, rows), bf16),
                pltpu.VMEM((keys, rows), bf16),
                pltpu.VMEM((window, 128), f32),
                pltpu.VMEM((window, 128), f32),
            ],
        ),
        out_shape=[
            jax.ShapeDtypeStruct((128, GROUP_COLS), bf16),
            jax.ShapeDtypeStruct((128, GROUP_COLS), bf16),
            jax.ShapeDtypeStruct((256, 256), bf16),
            jax.ShapeDtypeStruct((256, 256), bf16),
            jax.ShapeDtypeStruct((256, 256), bf16),
            jax.ShapeDtypeStruct((256, 256), bf16),
            jax.ShapeDtypeStruct((256, 256), f32),
        ],
        compiler_params=pltpu.CompilerParams(
            dimension_semantics=("arbitrary", "arbitrary"), vmem_limit_bytes=56 * 1024 * 1024
        ),
        cost_estimate=pl.CostEstimate(
            flops=12 * 2 * 16 * 128 * keys * 128,
            bytes_accessed=5 << 20,
            transcendentals=32 * 128 * keys,
        ),
    )(core, queries, grads, q_other, g_other, kv_own, *kv_halo, key_mark, query_mark)


def on_device(
    activations,
    queries,
    saved_keys,
    saved_values,
    output_gradient,
    segments,
    weight_codes,
    exponents,
):
    bf16, f32 = jnp.bfloat16, jnp.float32
    dp_size, seq_size = lax.axis_size("dp"), lax.axis_size("seq")
    dp_idx, seq_idx = lax.axis_index("dp"), lax.axis_index("seq")
    core = seq_idx % 2
    chip = seq_idx // 2
    chips = seq_size // 2
    same_core = [[2 * k + c for k in range(chips)] for c in range(2)]
    swap_cores = [(i, i ^ 1) for i in range(seq_size)]
    halo_chips = DOC_LIMIT // 256

    def head_cols(array, which, width):
        return lax.dynamic_slice_in_dim(array, which * width, width, 1)

    kv_mine = jnp.concatenate(
        [head_cols(saved_keys, core, 128), head_cols(saved_values, core, 128)], axis=1
    )
    kv_theirs = jnp.concatenate(
        [head_cols(saved_keys, 1 - core, 128), head_cols(saved_values, 1 - core, 128)], axis=1
    )
    rows_dev = weight_codes.shape[0]
    first_global = (dp_idx * seq_size + seq_idx) * rows_dev
    row_block = (first_global + jnp.arange(rows_dev)) // SCALE_BLOCK_SIDE
    row_pick = (row_block[:, None] == jnp.arange(exponents.shape[0])[None, :]).astype(f32)
    row_scale = jnp.dot(
        row_pick, jnp.exp2(exponents.astype(f32)), precision=lax.Precision.HIGHEST
    )
    column_scale = jnp.repeat(row_scale, SCALE_BLOCK_SIDE, axis=1)
    weight_rows = decode_rows(weight_codes, column_scale)
    x_size = 4
    x_at, z_at = dp_idx % x_size, dp_idx // x_size
    z_size = dp_size // x_size

    def x_turn(d):
        return [
            (i, i // x_size * x_size + (i % x_size + d) % x_size) for i in range(dp_size)
        ]

    def z_turn(d):
        return [(i, (i // x_size + d) % z_size * x_size + i % x_size) for i in range(dp_size)]

    widened = jnp.tile(weight_rows, (WIDEN, 1))
    kv_theirs, widened = lax.optimization_barrier((kv_theirs, widened))
    weight_block = (
        lax.all_gather(widened, "dp", axis=0, tiled=True)
        .reshape(dp_size, WIDEN, rows_dev, weight_rows.shape[1])[:, 0]
        .reshape(dp_size * rows_dev, weight_rows.shape[1])
    )

    kv_got = lax.ppermute(kv_theirs, "seq", swap_cores)
    kv_own = jnp.where(
        core == 0,
        jnp.concatenate([kv_mine, kv_got], axis=0),
        jnp.concatenate([kv_got, kv_mine], axis=0),
    )
    kv_halo = [
        lax.ppermute(kv_own, "seq", [(i, i + 2 * d) for i in range(seq_size - 2 * d)])
        for d in range(1, halo_chips + 1)
    ]
    q_other = lax.ppermute(head_cols(queries, 1 - core, GROUP_COLS), "seq", swap_cores)
    g_other = lax.ppermute(head_cols(output_gradient, 1 - core, GROUP_COLS), "seq", swap_cores)

    docs = segments[0]
    padded = jnp.concatenate([jnp.full((DOC_LIMIT,), 127, jnp.int32), docs])
    key_docs = lax.dynamic_slice_in_dim(padded, chip * 256, DOC_LIMIT + 256, 0)
    own_docs = lax.dynamic_slice_in_dim(docs, seq_idx * 128, 128, 0)
    other_docs = lax.dynamic_slice_in_dim(docs, (seq_idx + 1 - 2 * core) * 128, 128, 0)
    lanes = jnp.arange(128, dtype=jnp.int32)
    key_mark = (key_docs[:, None] == lanes[None, :]).astype(bf16)
    query_mark = jnp.where(
        jnp.stack([own_docs, other_docs])[:, :, None] == lanes[None, None, :], 0.0, masked_bias
    ).astype(bf16)

    tokens = activations.shape[0]
    piece = activations.shape[1] // (dp_size * seq_size)
    act_rows = (
        activations.T.reshape(dp_size, seq_size, piece, tokens)
        .transpose(1, 0, 2, 3)
        .reshape(seq_size, dp_size * piece, tokens)
    )
    act_rows, *kv_halo = lax.optimization_barrier((act_rows, *kv_halo))
    arrived = lax.all_to_all(act_rows, "seq", split_axis=0, concat_axis=0)

    dq_own, dq_other, *dkv_halo, dkv_own = attend_grads(
        core.reshape(1), queries, output_gradient, q_other, g_other, kv_own, kv_halo,
        key_mark, query_mark,
    )
    dq_back = lax.ppermute(dq_other, "seq", swap_cores)
    grad_q = jnp.where(
        core == 0,
        jnp.concatenate([dq_own, dq_back], axis=1),
        jnp.concatenate([dq_back, dq_own], axis=1),
    )

    arrived_now, dkv_own, *dkv_halo = lax.optimization_barrier((arrived, dkv_own, *dkv_halo))
    act_all = arrived_now.transpose(1, 0, 2).reshape(dp_size * piece, seq_size * tokens)
    kv_sum = dkv_own
    for d in range(1, halo_chips + 1):
        part = lax.ppermute(
            dkv_halo[d - 1], "seq", [(i, i - 2 * d) for i in range(2 * d, seq_size)]
        )
        kv_sum = kv_sum + part.astype(f32)
    kv_chip, weight_block, act_all, grad_q = lax.optimization_barrier(
        (kv_sum.astype(bf16), weight_block, act_all, grad_q)
    )
    kv_group = lax.all_to_all(
        jnp.broadcast_to(kv_chip[None], (chips,) + kv_chip.shape),
        "seq",
        split_axis=0,
        concat_axis=0,
        axis_index_groups=same_core,
    ).reshape(chips * 256, 256)
    kv_swap = lax.ppermute(kv_group, "seq", swap_cores)
    weight_part = jnp.concatenate(
        [dot(act_all, kv_group, NN), dot(act_all, kv_swap, NN)], axis=1
    ).astype(bf16)

    def ring_scatter(blocks, turn, size, at):
        total = lax.dynamic_index_in_dim(blocks, at, 0, keepdims=False).astype(f32)
        for d in range(1, size):
            block = lax.dynamic_index_in_dim(blocks, (at + d) % size, 0, keepdims=False)
            total = total + lax.ppermute(block.astype(bf16), "dp", turn(d)).astype(f32)
        return total

    blocks = weight_part.reshape(z_size, x_size, piece, weight_part.shape[1]).transpose(1, 0, 2, 3)
    kv_group, kv_swap, blocks = lax.optimization_barrier((kv_group, kv_swap, blocks))
    in_row = ring_scatter(blocks, x_turn, x_size, x_at)
    total = ring_scatter(in_row, z_turn, z_size, z_at)
    own_k, own_v, other_k, other_v = (total[:, i * 128 : (i + 1) * 128] for i in range(4))
    grad_weights = jnp.where(
        core == 0,
        jnp.concatenate([own_k, other_k, own_v, other_v], axis=1),
        jnp.concatenate([other_k, own_k, other_v, own_v], axis=1),
    )
    def cols_of(which):
        return jnp.concatenate(
            [head_cols(weight_block, which, 128), head_cols(weight_block, 2 + which, 128)], axis=1
        )

    grad_x_rows = (
        dot(cols_of(core), kv_group, NT) + dot(cols_of(1 - core), kv_swap, NT)
    ).astype(bf16)
    grad_x_rows = grad_x_rows.reshape(dp_size * piece, seq_size, tokens).transpose(1, 0, 2)
    grad_x = lax.all_to_all(grad_x_rows, "seq", split_axis=0, concat_axis=0)
    grad_x = (
        grad_x.reshape(seq_size, dp_size, piece, tokens)
        .transpose(1, 0, 2, 3)
        .reshape(dp_size * seq_size * piece, tokens)
        .T
    )
    return (grad_q, grad_x, grad_weights)


def solution(mesh):
    return jax.shard_map(
        on_device,
        mesh=mesh,
        in_specs=(
            P(("dp", "seq"), None),
            P(("dp", "seq"), None),
            P(("dp", "seq"), None),
            P(("dp", "seq"), None),
            P(("dp", "seq"), None),
            P("dp", None),
            P(("dp", "seq"), None),
            P(),
        ),
        out_specs=(P(("dp", "seq"), None), P(("dp", "seq"), None), P(("dp", "seq"), None)),
        check_vma=False,
    )
```
